1024 devices in a mesh: section: 8 (over y), seq: 8 (over z), dp: 16 (over x, core).
Axes of the slice: x: 8, y: 8, z: 8, core: 2. Of those that a mesh axis runs over, the one named last changes fastest.
Arguments:
- section_inputs: bfloat16 [8, 16, 1024, 2560], P('section', 'dp', 'seq'), may hold values from -6 to 6
- grad_send: bfloat16 [8, 16, 1024, 2560], P('section', 'dp', 'seq'), may hold values from -6 to 6
- gains: float32 [8, 3, 2560], P('section'), may hold values from -6 to 6
- layout: int32 [8, 8], P('section', 'seq'), may hold values 0 or 1
Outputs:
- input_grad: bfloat16 [8, 16, 1024, 2560], P('section', 'dp', 'seq')
- gain_grads: float32 [8, 3, 2560], P('section')
The draws below stay inside these ranges and needn't reach their ends.
All inputs are finite; a program needn't handle non-finite values. No bound on the sum of `layout` on one device may be relied on, other than what follows from the above.
Results may differ from the reference program's by a relative error of at most 0.02.
Values may be sent and summed in bfloat16 or wider, within the bound.
A program may use at most 32 MiB of HBM per device.

```python
import math
import jax
import jax.numpy as jnp
from jax import lax

D = 2560
HEAD_DIM = 128
BLK = 128
SECTIONS = 8
NB = 8
STRIDE = 4
SEQ_LEN = 1024
BATCH = 16


def draw_gains(key, part):
    key = jax.random.fold_in(key, 7)
    key_pair = jax.random.fold_in(key, 0)
    key_value = jax.random.fold_in(key, 3)
    pair_gains = jnp.clip(jax.random.normal(key_pair, (SECTIONS, 2, D), jnp.float32), -4.0, 4.0)
    query_gain = pair_gains[:, 0]
    key_gain = pair_gains[:, 1]
    value_gain = jnp.exp(jax.random.uniform(key_value, (SECTIONS, D), jnp.float32, math.log(0.5), math.log(3.0)))
    return jnp.stack([query_gain, key_gain, value_gain], axis=1)


def set_ends(values, rng, low, largest):
    longest = values.shape.index(max(values.shape))
    spots = []
    for shift in (0, 1):
        where = [jax.random.randint(jax.random.fold_in(rng, axis), (), 0, length) for axis, length in enumerate(values.shape)]
        where[longest] = (where[longest] + shift) % values.shape[longest]
        spots.append(tuple(where))
    return values.at[spots[0]].set(low).at[spots[1]].set(largest)


def block_scale(key, extent, cuts, smallest, high):
    def one(position, blocks):
        heights = jax.random.uniform(jax.random.fold_in(jax.random.fold_in(key, 6), position), (blocks,), jnp.float32, smallest / len(cuts), high / len(cuts))
        return jnp.repeat(jnp.exp(heights), extent[position] // blocks).reshape((-1,) + (1,) * (len(extent) - position - 1))

    loudness = one(*cuts[0])
    for cut in cuts[1:]:
        loudness = loudness * one(*cut)
    return loudness


def normal_values(key, shape, spread, limit, cuts=(), kind=jnp.bfloat16):
    result = jax.random.normal(key, shape, jnp.float32) * spread
    if len(cuts) > 0:
        result = block_scale(key, shape, cuts, -0.22, 0.18) * result
    return jnp.clip(result, min=-limit, max=limit).astype(kind)


def setup_inputs(seed: int = 0) -> dict:
    streams_of = jax.random.split(jax.random.key(seed), 5)
    section_inputs = normal_values(streams_of[0], (SECTIONS, BATCH, SEQ_LEN, D), 1.0, 6.0, ((0, 8), (1, 16), (2, 8)))
    grad_send = normal_values(streams_of[1], (SECTIONS, BATCH, SEQ_LEN, D), 1.0, 6.0, ((0, 8), (1, 16), (2, 8)))
    gains = draw_gains(jax.random.fold_in(streams_of[4], 71), 0)
    layout = set_ends((jax.random.randint(streams_of[3], (SECTIONS, NB), 0, 4) < 3).astype(jnp.int32), jax.random.fold_in(streams_of[3], 1), 0, 1)
    return dict(section_inputs=section_inputs, grad_send=grad_send, gains=gains, layout=layout)


EPS = 1e-06
NEG = -1e+30

def contract(form, left, right):
    return jnp.einsum(form, left.astype(jnp.float32), right.astype(jnp.float32), precision=lax.Precision.HIGHEST)

def normalize(inputs):
    input_float = inputs.astype(jnp.float32)
    scale_inv = lax.rsqrt(lax.optimization_barrier(jnp.mean(input_float * input_float, axis=-1, keepdims=True)) + EPS)
    return ((input_float * scale_inv).astype(jnp.bfloat16), scale_inv)

def project(normed, gain_row):
    return (normed.astype(jnp.float32) * gain_row).astype(jnp.bfloat16)

def heads_of(tensor, head_dim):
    return tensor.reshape(tensor.shape[0], tensor.shape[1], tensor.shape[2] // head_dim, head_dim)

def flatten(tensor):
    return tensor.reshape(tensor.shape[0], tensor.shape[1], tensor.shape[2] * tensor.shape[3])

def shift_blocks(tensor, amount):
    padding = jnp.zeros((abs(amount),) + tensor.shape[1:], tensor.dtype)
    if amount > 0:
        return jnp.concatenate([padding, tensor[:-amount]], axis=0)
    return jnp.concatenate([tensor[-amount:], padding], axis=0)

def weights_of(query_heads, key_heads, far_key_heads, usable, head_dim):
    factor = 1.0 / math.sqrt(head_dim)
    near_scores = contract('nthe,nuhe->nhtu', query_heads, key_heads) * factor
    far_scores = contract('nthe,nuhe->nhtu', query_heads, far_key_heads) * factor
    row_index = lax.broadcasted_iota(jnp.int32, near_scores.shape[-2:], 0)
    col_index = lax.broadcasted_iota(jnp.int32, near_scores.shape[-2:], 1)
    near_scores = jnp.where(row_index >= col_index, near_scores, NEG)
    far_scores = jnp.where(usable[:, None, None, None], far_scores, NEG)
    row_top = jnp.maximum(lax.optimization_barrier(jnp.max(near_scores, axis=-1, keepdims=True)), lax.optimization_barrier(jnp.max(far_scores, axis=-1, keepdims=True)))
    near_exp = jnp.exp(near_scores - row_top)
    far_exp = jnp.exp(far_scores - row_top)
    row_total = lax.optimization_barrier(jnp.sum(near_exp, axis=-1, keepdims=True)) + lax.optimization_barrier(jnp.sum(far_exp, axis=-1, keepdims=True))
    return (near_exp / row_total, far_exp / row_total)

def attention_grads(queries, keys_own, values_own, keys_far, values_far, grad_out, usable, head_dim):
    query_heads = heads_of(queries, head_dim)
    key_heads = heads_of(keys_own, head_dim)
    value_heads = heads_of(values_own, head_dim)
    far_key_heads = heads_of(keys_far, head_dim)
    far_value_heads = heads_of(values_far, head_dim)
    grad_heads = heads_of(grad_out, head_dim)
    near_prob, far_prob = weights_of(query_heads, key_heads, far_key_heads, usable, head_dim)
    near_dprob = contract('nthe,nuhe->nhtu', grad_heads, value_heads)
    far_dprob = contract('nthe,nuhe->nhtu', grad_heads, far_value_heads)
    row_delta = lax.optimization_barrier(jnp.sum(near_prob * near_dprob, axis=-1, keepdims=True)) + lax.optimization_barrier(jnp.sum(far_prob * far_dprob, axis=-1, keepdims=True))
    factor = 1.0 / math.sqrt(head_dim)
    near_dscore = (near_prob * (near_dprob - row_delta) * factor).astype(jnp.bfloat16)
    far_dscore = (far_prob * (far_dprob - row_delta) * factor).astype(jnp.bfloat16)
    d_query = contract('nhtu,nuhe->nthe', near_dscore, key_heads) + contract('nhtu,nuhe->nthe', far_dscore, far_key_heads)
    d_key_own = contract('nhtu,nthe->nuhe', near_dscore, query_heads)
    d_key_far = contract('nhtu,nthe->nuhe', far_dscore, query_heads).astype(jnp.bfloat16)
    d_value_own = contract('nhtu,nthe->nuhe', near_prob.astype(jnp.bfloat16), grad_heads)
    d_value_far = contract('nhtu,nthe->nuhe', far_prob.astype(jnp.bfloat16), grad_heads).astype(jnp.bfloat16)
    return (flatten(d_query), flatten(d_key_own), flatten(d_value_own), flatten(d_key_far), flatten(d_value_far))

def finish(inputs, normed, scale_inv, grad_out, d_query, d_key, d_value, gain_rows):
    d_normed = d_query * gain_rows[0] + d_key * gain_rows[1] + d_value * gain_rows[2]
    input_float = inputs.astype(jnp.float32)
    input_grad = (grad_out.astype(jnp.float32) + scale_inv * d_normed - input_float * scale_inv ** 3 * lax.optimization_barrier(jnp.mean(d_normed * input_float, axis=-1, keepdims=True))).astype(jnp.bfloat16)
    normed_float = normed.astype(jnp.float32)
    terms = jnp.stack([lax.optimization_barrier(jnp.sum(d_query * normed_float, axis=(0, 1))), lax.optimization_barrier(jnp.sum(d_key * normed_float, axis=(0, 1))), lax.optimization_barrier(jnp.sum(d_value * normed_float, axis=(0, 1)))])
    return (input_grad, terms)

def reference(section_inputs, grad_send, gains, layout):
    grads_list = []
    gain_list = []
    block_index = jnp.arange(NB)
    for section_index in range(SECTIONS):
        gain_rows = gains[section_index]
        usable = (block_index >= STRIDE) & (layout[section_index] == 1)
        cotangent = grad_send[(section_index + 1) % SECTIONS]

        def per_row(packed, gain_rows=gain_rows, usable=usable):
            inputs = packed[0].reshape(NB, BLK, D)
            grad_out = packed[1].reshape(NB, BLK, D)
            normed, scale_inv = normalize(inputs)
            queries = project(normed, gain_rows[0])
            keys_own = project(normed, gain_rows[1])
            values_own = project(normed, gain_rows[2])
            keys_far = shift_blocks(keys_own, STRIDE)
            values_far = shift_blocks(values_own, STRIDE)
            grads = attention_grads(queries, keys_own, values_own, keys_far, values_far, grad_out, usable, HEAD_DIM)
            d_key = grads[1] + shift_blocks(grads[3], -STRIDE).astype(jnp.float32)
            d_value = grads[2] + shift_blocks(grads[4], -STRIDE).astype(jnp.float32)
            input_grad, terms = finish(inputs, normed, scale_inv, grad_out, grads[0], d_key, d_value, gain_rows)
            return (input_grad.reshape(SEQ_LEN, D), terms)
        row_grads, row_terms = lax.map(per_row, (section_inputs[section_index], cotangent))
        grads_list.append(row_grads)
        gain_list.append(lax.optimization_barrier(jnp.sum(row_terms, axis=0)) / math.sqrt(BATCH * SEQ_LEN))
    return (jnp.stack(grads_list), jnp.stack(gain_list))
```

```python
import math

import jax
import jax.numpy as jnp
from jax import lax
from jax.experimental import pallas as pl
from jax.experimental.pallas import tpu as pltpu
from jax.sharding import PartitionSpec as P

MESH = pl.DeviceIdType.MESH
HEAD = 128
EPS = 1e-06
NEG = -1e30
PER = 2
F32 = jnp.float32
BF16 = jnp.bfloat16


def dot(left, right, dims):
    return lax.dot_general(left, right, (dims, ((), ())), preferred_element_type=F32)


def make_kernel(n_seq, n_dp, n_section, channels, block):
    heads = channels // HEAD
    chunks = heads // PER
    width = PER * HEAD
    half = n_seq // 2
    owners = n_dp // 2
    tokens_all = n_dp * n_seq * block
    factor = 1.0 / math.sqrt(HEAD)

    def kernel(
        layout_ref, x_hbm, g_hbm, gains_hbm, out_hbm, gain_out,
        xv, gv, gains, nrm, far, rsend, rrecv, dn, scale, macc, ov,
        gg, rsbuf, zlow, zbuf, fin,
        load_sem, out_sem, g_s, g_r, f_s, f_r, r_s, r_r,
        rs_s, rs_r, zl_s, zl_r, z_s, z_r, ag_s, ag_r,
    ):
        z = lax.axis_index("seq")
        d = lax.axis_index("dp")
        s = lax.axis_index("section")
        high = z >= half
        low = z < half
        partner = lax.rem(z + half, n_seq)
        slot = lax.rem(z, half)
        owner = lax.rem(d, 2) == 0
        piece = d // 2
        below = lax.rem(s + n_section - 1, n_section)
        above = lax.rem(s + 1, n_section)

        def remote(src, dst, send, recv, where):
            return pltpu.make_async_remote_copy(
                src_ref=src, dst_ref=dst, send_sem=send, recv_sem=recv,
                device_id=where, device_id_type=MESH,
            )

        bar = pltpu.get_barrier_semaphore()

        def greet(where):
            pl.semaphore_signal(bar, inc=1, device_id=where, device_id_type=MESH)

        @pl.when(high)
        def _():
            greet({"seq": partner})

        load_x = pltpu.make_async_copy(x_hbm.at[0, 0], xv, load_sem.at[0])
        load_x.start()
        load_gains = pltpu.make_async_copy(gains_hbm.at[0], gains, load_sem.at[1])
        load_gains.start()
        greet({"section": above})

        @pl.when(high)
        def _():
            for j in range(half):
                @pl.when(z != half + j)
                def _():
                    greet({"seq": half + j})

        @pl.when(low)
        def _():
            for j in range(half):
                greet({"seq": half + j})

        for p in range(n_dp):
            if p % 2 == 0:
                @pl.when(d != p)
                def _():
                    greet({"dp": p})
            else:
                @pl.when(owner)
                def _():
                    greet({"dp": p})

        def lanes(h):
            return pl.ds(pl.multiple_of(h * HEAD, HEAD), HEAD)

        load_x.wait()
        load_gains.wait()

        def square(h, acc):
            v = xv[:, lanes(h)].astype(F32)
            return acc + v * v

        squares = lax.fori_loop(0, heads, square, jnp.zeros((block, HEAD), F32))
        mean = jnp.sum(squares, axis=1, keepdims=True) / channels
        scale[...] = jnp.broadcast_to(lax.rsqrt(mean + EPS), (block, HEAD))

        def norm(h, _):
            nrm[h] = (xv[:, lanes(h)].astype(F32) * scale[...]).astype(BF16)
            return 0

        lax.fori_loop(0, heads, norm, 0)
        macc[...] = jnp.zeros_like(macc)
        gg[...] = jnp.zeros_like(gg)

        dp_waits = jnp.where(owner, n_dp - 1, owners)
        pl.semaphore_wait(bar, jnp.where(high, 2 * half - 1, 1) + 1 + dp_waits)

        def far_copy(c):
            part = pl.ds(c * PER, PER)
            return remote(nrm.at[part], far.at[part], f_s.at[c], f_r.at[c], {"seq": partner})

        def ret_copy(c):
            part = pl.ds(c * PER, PER)
            return remote(rsend.at[part], rrecv.at[part], r_s.at[c], r_r.at[c], {"seq": partner})

        def g_copy(c):
            part = pl.ds(pl.multiple_of(c * width, width), width)
            return remote(
                g_hbm.at[0, 0, :, part], gv.at[:, part], g_s.at[c], g_r.at[c], {"section": below}
            )

        @pl.when(low)
        def _():
            def send(c, _):
                far_copy(c).start()
                return 0

            lax.fori_loop(0, chunks, send, 0)

        def send_g(c, _):
            g_copy(c).start()
            return 0

        lax.fori_loop(0, chunks, send_g, 0)

        def head(h, with_far):
            part = lanes(h)
            g0 = gains[pl.ds(0, 1), part]
            g1 = gains[pl.ds(1, 1), part]
            g2 = gains[pl.ds(2, 1), part]
            n = nrm[h].astype(F32)
            q = (n * g0).astype(BF16)
            k = (n * g1).astype(BF16)
            v = (n * g2).astype(BF16)
            cot = gv[:, part]
            key = lax.broadcasted_iota(jnp.int32, (block, block), 0)
            query = lax.broadcasted_iota(jnp.int32, (block, block), 1)
            if with_far:
                nf = far[h].astype(F32)
                k = jnp.concatenate([k, (nf * g1).astype(BF16)], axis=0)
                v = jnp.concatenate([v, (nf * g2).astype(BF16)], axis=0)
            scores = dot(k, q, ((1,), (1,))) * factor
            dprobs = dot(v, cot, ((1,), (1,)))
            near = jnp.where(key <= query, scores[:block], NEG)
            if with_far:
                usable = jnp.full((block, block), layout_ref[0, 0], jnp.int32) == 1
                scores = jnp.concatenate([near, jnp.where(usable, scores[block:], NEG)], axis=0)
            else:
                scores = near
            top = jnp.max(scores, axis=0, keepdims=True)
            weights = jnp.exp(scores - top)
            probs = weights * (1.0 / jnp.sum(weights, axis=0, keepdims=True))
            delta = jnp.sum(probs * dprobs, axis=0, keepdims=True)
            dscores = (probs * (dprobs - delta) * factor).astype(BF16)
            d_query = dot(dscores, k, ((0,), (0,)))
            d_key = dot(dscores, q, ((1,), (0,)))
            d_value = dot(probs.astype(BF16), cot, ((1,), (0,)))
            own_key, own_value = d_key[:block], d_value[:block]
            key_terms = own_key * n
            value_terms = own_value * n
            if with_far:
                far_key, far_value = d_key[block:], d_value[block:]
                key_terms += far_key * nf
                value_terms += far_value * nf
                rsend[h] = (far_key * g1 + far_value * g2).astype(BF16)
            gg[pl.ds(3 * h, 1), :] = jnp.sum(d_query * n, axis=0, keepdims=True)
            gg[pl.ds(3 * h + 1, 1), :] = jnp.sum(key_terms, axis=0, keepdims=True)
            gg[pl.ds(3 * h + 2, 1), :] = jnp.sum(value_terms, axis=0, keepdims=True)
            d_normed = d_query * g0 + own_key * g1 + own_value * g2
            dn[h] = d_normed
            return d_normed * xv[:, part].astype(F32)

        def rs_copy(p, source_slot):
            return remote(
                gg.at[pl.ds(8 * p, 8)], rsbuf.at[source_slot], rs_s.at[p], rs_r.at[source_slot],
                {"dp": 2 * p},
            )

        def rs_send():
            for p in range(owners):
                @pl.when(d != 2 * p)
                def _():
                    rs_copy(p, d).start()

                @pl.when(d == 2 * p)
                def _():
                    rsbuf[2 * p] = gg[pl.ds(8 * p, 8), :]

        def rs_sum():
            for p in range(n_dp):
                @pl.when(d != p)
                def _():
                    rs_copy(0, p).wait_recv()
            return jnp.sum(rsbuf[...], axis=0)

        def rs_wait_send():
            for p in range(owners):
                @pl.when(d != 2 * p)
                def _():
                    rs_copy(p, d).wait_send()

        zl_copy = remote(zlow.at[0], zlow.at[1], zl_s, zl_r, {"seq": partner})

        def z_copy(j, source):
            return remote(zbuf.at[source], zbuf.at[source], z_s.at[j], z_r.at[source], {"seq": j})

        def ag_copy(p, source):
            return remote(fin.at[source], fin.at[source], ag_s.at[p], ag_r.at[source], {"dp": p})

        def gather_start():
            for j in range(half):
                @pl.when(z != half + j)
                def _():
                    z_copy(0, j).wait_recv()
            fin[piece] = jnp.sum(zbuf[...], axis=0) * (1.0 / math.sqrt(tokens_all))
            for p in range(n_dp):
                @pl.when(d != p)
                def _():
                    ag_copy(p, piece).start()

        def gather_end():
            for p in range(owners):
                @pl.when(d != 2 * p)
                def _():
                    ag_copy(0, p).wait_recv()
            for h in range(heads):
                for r in range(3):
                    row = 3 * h + r
                    gain_out[0, pl.ds(r, 1), pl.ds(h * HEAD, HEAD)] = fin[
                        row // 8, pl.ds(row % 8, 1), :
                    ]

            @pl.when(owner)
            def _():
                for p in range(n_dp):
                    @pl.when(d != p)
                    def _():
                        ag_copy(p, piece).wait_send()

        def out_copy(c):
            part = pl.ds(pl.multiple_of(c * width, width), width)
            return pltpu.make_async_copy(
                ov.at[:, part], out_hbm.at[0, 0, :, part], out_sem.at[c]
            )

        def finish():
            inv = scale[...]
            total = jnp.sum(macc[...], axis=1, keepdims=True) / channels
            pull = inv * inv * inv * total

            def body(c, _):
                for i in range(PER):
                    h = c * PER + i
                    part = lanes(h)
                    ov[:, part] = (
                        gv[:, part].astype(F32) + inv * dn[h] - xv[:, part].astype(F32) * pull
                    ).astype(BF16)
                out_copy(c).start()
                return 0

            lax.fori_loop(0, chunks, body, 0)

        @pl.when(low)
        def _():
            def near(c, _):
                g_copy(c).wait_recv()
                add = head(c * PER, False)
                for i in range(1, PER):
                    add += head(c * PER + i, False)
                macc[...] += add
                return 0

            lax.fori_loop(0, chunks, near, 0)
            rs_send()

            @pl.when(owner)
            def _():
                zlow[0] = rs_sum()
                zl_copy.start()

            def back(c, _):
                ret_copy(c).wait_recv()
                for i in range(PER):
                    h = c * PER + i
                    more = rrecv[h].astype(F32)
                    dn[h] += more
                    macc[...] += more * xv[:, lanes(h)].astype(F32)
                return 0

            lax.fori_loop(0, chunks, back, 0)
            finish()

            @pl.when(owner)
            def _():
                gather_start()

            gather_end()

            @pl.when(owner)
            def _():
                zl_copy.wait_send()

            def sent(c, _):
                far_copy(c).wait_send()
                return 0

            lax.fori_loop(0, chunks, sent, 0)

        @pl.when(high)
        def _():
            def both(c, _):
                g_copy(c).wait_recv()
                far_copy(c).wait_recv()
                add = head(c * PER, True)
                for i in range(1, PER):
                    add += head(c * PER + i, True)
                ret_copy(c).start()
                macc[...] += add
                return 0

            lax.fori_loop(0, chunks, both, 0)
            rs_send()

            @pl.when(owner)
            def _():
                mine = rs_sum()
                zl_copy.wait_recv()
                zbuf[slot] = mine + zlow[1]
                for j in range(n_seq):
                    @pl.when(z != j)
                    def _():
                        z_copy(j, slot).start()
                gather_start()

            finish()
            gather_end()

            @pl.when(owner)
            def _():
                for j in range(n_seq):
                    @pl.when(z != j)
                    def _():
                        z_copy(j, slot).wait_send()

            def sent(c, _):
                ret_copy(c).wait_send()
                return 0

            lax.fori_loop(0, chunks, sent, 0)

        rs_wait_send()

        def last(c, _):
            g_copy(c).wait_send()
            out_copy(c).wait()
            return 0

        lax.fori_loop(0, chunks, last, 0)

    dma = pltpu.SemaphoreType.DMA
    scratch = [
        pltpu.VMEM((block, channels), BF16),
        pltpu.VMEM((block, channels), BF16),
        pltpu.VMEM((3, channels), F32),
        pltpu.VMEM((heads, block, HEAD), BF16),
        pltpu.VMEM((heads, block, HEAD), BF16),
        pltpu.VMEM((heads, block, HEAD), BF16),
        pltpu.VMEM((heads, block, HEAD), BF16),
        pltpu.VMEM((heads, block, HEAD), F32),
        pltpu.VMEM((block, HEAD), F32),
        pltpu.VMEM((block, HEAD), F32),
        pltpu.VMEM((block, channels), BF16),
        pltpu.VMEM((8 * owners, HEAD), F32),
        pltpu.VMEM((n_dp, 8, HEAD), F32),
        pltpu.VMEM((2, 8, HEAD), F32),
        pltpu.VMEM((half, 8, HEAD), F32),
        pltpu.VMEM((owners, 8, HEAD), F32),
        dma((2,)), dma((chunks,)),
        dma((chunks,)), dma((chunks,)), dma((chunks,)), dma((chunks,)),
        dma((chunks,)), dma((chunks,)),
        dma((owners,)), dma((n_dp,)), dma(()), dma(()),
        dma((n_seq,)), dma((half,)), dma((n_dp,)), dma((owners,)),
    ]
    return pl.pallas_call(
        kernel,
        out_shape=(
            jax.ShapeDtypeStruct((1, 1, block, channels), BF16),
            jax.ShapeDtypeStruct((1, 3, channels), F32),
        ),
        in_specs=[
            pl.BlockSpec(memory_space=pltpu.SMEM),
            pl.BlockSpec(memory_space=pl.ANY),
            pl.BlockSpec(memory_space=pl.ANY),
            pl.BlockSpec(memory_space=pl.ANY),
        ],
        out_specs=(
            pl.BlockSpec(memory_space=pl.ANY),
            pl.BlockSpec(memory_space=pltpu.VMEM),
        ),
        scratch_shapes=scratch,
        compiler_params=pltpu.CompilerParams(
            collective_id=0, has_side_effects=True, vmem_limit_bytes=32 << 20
        ),
    )


def solution(mesh):
    def local(section_inputs, grad_send, gains, layout):
        call = make_kernel(
            mesh.shape["seq"], mesh.shape["dp"], mesh.shape["section"],
            section_inputs.shape[-1], section_inputs.shape[-2],
        )
        return call(layout, section_inputs, grad_send, gains)

    in_specs = (
        P("section", "dp", "seq", None),
        P("section", "dp", "seq", None),
        P("section", None, None),
        P("section", "seq"),
    )
    out_specs = (P("section", "dp", "seq", None), P("section", None, None))
    return jax.shard_map(local, mesh=mesh, in_specs=in_specs, out_specs=out_specs, check_vma=False)
```

```python
import math

import jax
import jax.numpy as jnp
from jax import lax
from jax.experimental import pallas as pl
from jax.experimental.pallas import tpu as pltpu
from jax.sharding import PartitionSpec as P

MESH = pl.DeviceIdType.MESH
HEAD = 128
EPS = 1e-06
NEG = -1e30
PER = 2
FORWARD = 8
GROUPS = ((0, 4), (4, 7), (7, 8), (0, 8), (8, 10))
HIGH_GROUPS, LOW_GROUPS = (0, 1, 2), (3, 4)
F32 = jnp.float32
BF16 = jnp.bfloat16


def dot(left, right, dims):
    return lax.dot_general(left, right, (dims, ((), ())), preferred_element_type=F32)


def make_kernel(n_seq, n_dp, n_section, channels, block):
    heads = channels // HEAD
    chunks = heads // PER
    moved = chunks - FORWARD
    width = PER * HEAD
    half = n_seq // 2
    chips = n_dp // 2
    groups = len(GROUPS)
    tokens_all = n_dp * n_seq * block
    factor = 1.0 / math.sqrt(HEAD)

    def kernel(
        layout_hbm, x_hbm, g_hbm, gains_hbm, out_hbm, gain_out,
        layout, xv, gv, gains, nrm, far, rsend, rrecv, nq, gq, msend, mrecv, flag,
        dn, scale, macc, ov, gg, zbuf, pair, xbuf, fin,
        load_sem, out_sem, g_s, g_r, f_s, f_r, r_s, r_r,
        nq_s, nq_r, gq_s, gq_r, m_s, m_r, one_s, one_r, z_s, z_r, sib_s, sib_r, x_s, x_r,
    ):
        z = lax.axis_index("seq")
        d = lax.axis_index("dp")
        s = lax.axis_index("section")
        high = z >= half
        low = z < half
        partner = lax.rem(z + half, n_seq)
        chip = d // 2
        core = lax.rem(d, 2)
        sibling = 2 * chip + 1 - core
        below = lax.rem(s + n_section - 1, n_section)
        above = lax.rem(s + 1, n_section)

        def remote(src, dst, send, recv, where):
            return pltpu.make_async_remote_copy(
                src_ref=src, dst_ref=dst, send_sem=send, recv_sem=recv,
                device_id=where, device_id_type=MESH,
            )

        bar = pltpu.get_barrier_semaphore()

        def greet(where):
            pl.semaphore_signal(bar, inc=1, device_id=where, device_id_type=MESH)

        greet({"seq": partner})
        load_x = pltpu.make_async_copy(x_hbm.at[0, 0], xv, load_sem.at[0])
        load_x.start()
        load_gains = pltpu.make_async_copy(gains_hbm, gains, load_sem.at[1])
        load_gains.start()
        load_layout = pltpu.make_async_copy(layout_hbm, layout, load_sem.at[2])
        load_layout.start()
        greet({"section": above})
        greet({"dp": sibling})
        for p in range(chips):
            @pl.when(chip != p)
            def _():
                greet({"dp": 2 * p + core})

        @pl.when(low)
        def _():
            greet({"section": above, "seq": partner})
            for j in range(half):
                @pl.when(z != j)
                def _():
                    greet({"seq": j})
                    greet({"seq": half + j})

        def lanes(h):
            return pl.ds(pl.multiple_of(h * HEAD, HEAD), HEAD)

        def wide(c):
            return pl.ds(pl.multiple_of(c * width, width), width)

        load_x.wait()

        def square(h, acc):
            v = xv[:, lanes(h)].astype(F32)
            return acc + v * v

        squares = lax.fori_loop(0, heads, square, jnp.zeros((block, HEAD), F32))
        mean = jnp.sum(squares, axis=1, keepdims=True) / channels
        scale[...] = jnp.broadcast_to(lax.rsqrt(mean + EPS), (block, HEAD))

        def norm(h, _):
            nrm[h] = (xv[:, lanes(h)].astype(F32) * scale[...]).astype(BF16)
            return 0

        lax.fori_loop(0, heads, norm, 0)
        load_gains.wait()
        load_layout.wait()
        flag[0] = jnp.full((8, HEAD), layout[0, 0], jnp.int32).astype(F32)
        macc[...] = jnp.zeros_like(macc)
        gg[...] = jnp.zeros_like(gg)

        pl.semaphore_wait(bar, jnp.where(high, half + 2, half + 1) + chips)

        def far_copy(c):
            part = pl.ds(c * PER, PER)
            return remote(nrm.at[part], far.at[part], f_s.at[c], f_r.at[c], {"seq": partner})

        def ret_copy(c):
            part = pl.ds(c * PER, PER)
            return remote(rsend.at[part], rrecv.at[part], r_s.at[c], r_r.at[c], {"seq": partner})

        def nq_copy(m):
            return remote(
                nrm.at[pl.ds((FORWARD + m) * PER, PER)], nq.at[pl.ds(m * PER, PER)],
                nq_s.at[m], nq_r.at[m], {"seq": partner},
            )

        def gq_copy(m):
            return remote(
                g_hbm.at[0, 0, :, wide(FORWARD + m)], gq.at[:, wide(m)],
                gq_s.at[m], gq_r.at[m], {"section": below, "seq": partner},
            )

        def back_copy(m):
            part = pl.ds(m * PER, PER)
            return remote(msend.at[part], mrecv.at[part], m_s.at[m], m_r.at[m], {"seq": partner})

        def g_copy(c):
            part = wide(c)
            return remote(
                g_hbm.at[0, 0, :, part], gv.at[:, part], g_s.at[c], g_r.at[c], {"section": below}
            )

        flag_copy = remote(flag.at[0], flag.at[1], one_s.at[0], one_r.at[0], {"seq": partner})
        total_copy = remote(fin, fin, one_s.at[1], one_r.at[1], {"seq": partner})

        @pl.when(low)
        def _():
            def send(c, _):
                far_copy(c).start()
                return 0

            lax.fori_loop(0, FORWARD, send, 0)

        @pl.when(high)
        def _():
            flag_copy.start()

            def send(m, _):
                nq_copy(m).start()
                gq_copy(m).start()
                return 0

            lax.fori_loop(0, moved, send, 0)

        def send_g(c, _):
            g_copy(c).start()
            return 0

        lax.fori_loop(0, chunks, send_g, 0)

        def head(h, own, cot, other=None, flags=None):
            part = lanes(h)
            g0 = gains[0, :, part]
            g1 = gains[1, :, part]
            g2 = gains[2, :, part]
            n = own.astype(F32)
            q = (n * g0).astype(BF16)
            k = (n * g1).astype(BF16)
            v = (n * g2).astype(BF16)
            key = lax.broadcasted_iota(jnp.int32, (block, block), 0)
            query = lax.broadcasted_iota(jnp.int32, (block, block), 1)
            if other is not None:
                nf = other.astype(F32)
                k = jnp.concatenate([k, (nf * g1).astype(BF16)], axis=0)
                v = jnp.concatenate([v, (nf * g2).astype(BF16)], axis=0)
            scores = dot(k, q, ((1,), (1,))) * factor
            dprobs = dot(v, cot, ((1,), (1,)))
            near = jnp.where(key <= query, scores[:block], NEG)
            if other is not None:
                scores = jnp.concatenate([near, jnp.where(flags > 0.5, scores[block:], NEG)], axis=0)
            else:
                scores = near
            top = jnp.max(scores, axis=0, keepdims=True)
            weights = jnp.exp(scores - top)
            probs = weights * (1.0 / jnp.sum(weights, axis=0, keepdims=True))
            delta = jnp.sum(probs * dprobs, axis=0, keepdims=True)
            dscores = (probs * (dprobs - delta) * factor).astype(BF16)
            d_query = dot(dscores, k, ((0,), (0,)))
            d_key = dot(dscores, q, ((1,), (0,)))
            d_value = dot(probs.astype(BF16), cot, ((1,), (0,)))
            own_key, own_value = d_key[:block], d_value[:block]
            key_terms = own_key * n
            value_terms = own_value * n
            d_far = None
            if other is not None:
                far_key, far_value = d_key[block:], d_value[block:]
                key_terms += far_key * nf
                value_terms += far_value * nf
                d_far = far_key * g1 + far_value * g2
            sums = [
                jnp.sum(term, axis=0, keepdims=True) for term in (d_query * n, key_terms, value_terms)
            ]
            return d_query * g0 + own_key * g1 + own_value * g2, d_far, sums

        def put_sums(c, i, sums):
            for r in range(3):
                gg[c, pl.ds(3 * i + r, 1), :] = sums[r]

        def x_of(h):
            return xv[:, lanes(h)].astype(F32)

        def tiles_of(k):
            return pl.ds(GROUPS[k][0], GROUPS[k][1] - GROUPS[k][0])

        def sib_copy(k):
            part = tiles_of(k)
            return remote(gg.at[part], pair.at[part], sib_s.at[k], sib_r.at[k], {"dp": sibling})

        def x_copy(k, p, source):
            part = tiles_of(k)
            return remote(
                xbuf.at[source, part], xbuf.at[source, part],
                x_s.at[k, p], x_r.at[k, source], {"dp": 2 * p + core},
            )

        def z_copy(k, j, source):
            part = tiles_of(k)
            return remote(
                zbuf.at[source, part], zbuf.at[source, part],
                z_s.at[k, j], z_r.at[k, source], {"seq": j},
            )

        def over_cores(k):
            part = tiles_of(k)
            sib_copy(k).wait_recv()
            xbuf[chip, part] = gg[part] + pair[part]
            for p in range(chips):
                @pl.when(chip != p)
                def _():
                    x_copy(k, p, chip).start()

        def over_x(k):
            part = tiles_of(k)
            for p in range(chips):
                @pl.when(chip != p)
                def _():
                    x_copy(k, 0, p).wait_recv()
            zbuf[z, part] = jnp.sum(xbuf[:, part], axis=0)
            for j in range(half):
                @pl.when(z != j)
                def _():
                    z_copy(k, j, z).start()

        def over_z():
            for k in HIGH_GROUPS:
                for j in range(half, n_seq):
                    z_copy(k, 0, j).wait_recv()
            for k in LOW_GROUPS:
                for j in range(half):
                    @pl.when(z != j)
                    def _():
                        z_copy(k, 0, j).wait_recv()
            ratio = 1.0 / math.sqrt(tokens_all)
            fin[pl.ds(0, FORWARD)] = jnp.sum(zbuf[:, pl.ds(0, FORWARD)], axis=0) * ratio
            fin[pl.ds(FORWARD, moved)] = (
                jnp.sum(zbuf[pl.ds(0, half), pl.ds(FORWARD, moved)], axis=0) * ratio
            )

        def sums_sent(k):
            sib_copy(k).wait_send()
            for p in range(chips):
                @pl.when(chip != p)
                def _():
                    x_copy(k, p, chip).wait_send()
            for j in range(half):
                @pl.when(z != j)
                def _():
                    z_copy(k, j, z).wait_send()

        def write_gains():
            for c in range(chunks):
                for i in range(PER):
                    for r in range(3):
                        part = pl.ds((c * PER + i) * HEAD, HEAD)
                        gain_out[r, :, part] = fin[c, pl.ds(3 * i + r, 1), :]

        def out_copy(c):
            part = wide(c)
            return pltpu.make_async_copy(
                ov.at[:, part], out_hbm.at[0, 0, :, part], out_sem.at[c]
            )

        def finish():
            inv = scale[...]
            total = jnp.sum(macc[...], axis=1, keepdims=True) / channels
            pull = inv * inv * inv * total

            def body(c, _):
                for i in range(PER):
                    h = c * PER + i
                    part = lanes(h)
                    ov[:, part] = (
                        gv[:, part].astype(F32) + inv * dn[h] - x_of(h) * pull
                    ).astype(BF16)
                out_copy(c).start()
                return 0

            lax.fori_loop(0, chunks, body, 0)

        @pl.when(low)
        def _():
            def near(c, _):
                g_copy(c).wait_recv()
                add = macc[...]
                for i in range(PER):
                    h = c * PER + i
                    grad, _far, sums = head(h, nrm[h], gv[:, lanes(h)])
                    dn[h] = grad
                    put_sums(c, i, sums)
                    add += grad * x_of(h)
                macc[...] = add
                return 0

            lax.fori_loop(0, chunks, near, 0)
            sib_copy(LOW_GROUPS[0]).start()
            flag_copy.wait_recv()

            def mine(m, _):
                nq_copy(m).wait_recv()
                gq_copy(m).wait_recv()
                add = macc[...]
                c = FORWARD + m
                for i in range(PER):
                    h = c * PER + i
                    grad, d_far, sums = head(
                        h, nq[m * PER + i], gq[:, lanes(m * PER + i)], nrm[h], flag[1, pl.ds(0, 1), :]
                    )
                    msend[m * PER + i] = grad.astype(BF16)
                    dn[h] += d_far
                    put_sums(c, i, [gg[c, pl.ds(3 * i + r, 1), :] + sums[r] for r in range(3)])
                    add += d_far * x_of(h)
                back_copy(m).start()
                macc[...] = add
                return 0

            lax.fori_loop(0, moved, mine, 0)
            sib_copy(LOW_GROUPS[1]).start()
            for k in LOW_GROUPS:
                over_cores(k)
            for k in LOW_GROUPS:
                over_x(k)

            def back(c, _):
                ret_copy(c).wait_recv()
                add = macc[...]
                for i in range(PER):
                    h = c * PER + i
                    more = rrecv[h].astype(F32)
                    dn[h] += more
                    add += more * x_of(h)
                macc[...] = add
                return 0

            lax.fori_loop(0, FORWARD, back, 0)
            finish()
            over_z()
            total_copy.start()
            write_gains()

            def sent(c, _):
                far_copy(c).wait_send()
                return 0

            lax.fori_loop(0, FORWARD, sent, 0)

            def given(m, _):
                back_copy(m).wait_send()
                return 0

            lax.fori_loop(0, moved, given, 0)
            for k in LOW_GROUPS:
                sums_sent(k)
            total_copy.wait_send()

        @pl.when(high)
        def _():
            def both(c, _):
                g_copy(c).wait_recv()
                far_copy(c).wait_recv()
                add = macc[...]
                for i in range(PER):
                    h = c * PER + i
                    grad, d_far, sums = head(
                        h, nrm[h], gv[:, lanes(h)], far[h], flag[0, pl.ds(0, 1), :]
                    )
                    dn[h] = grad
                    rsend[h] = d_far.astype(BF16)
                    put_sums(c, i, sums)
                    add += grad * x_of(h)
                ret_copy(c).start()
                macc[...] = add

                @pl.when(c == GROUPS[0][1] - 1)
                def _():
                    sib_copy(0).start()

                @pl.when(c == GROUPS[0][1])
                def _():
                    over_cores(0)

                @pl.when(c == GROUPS[1][1] - 1)
                def _():
                    sib_copy(1).start()

                return 0

            lax.fori_loop(0, FORWARD, both, 0)
            sib_copy(2).start()
            over_cores(1)
            over_cores(2)
            for k in HIGH_GROUPS:
                over_x(k)

            def theirs(m, _):
                back_copy(m).wait_recv()
                g_copy(FORWARD + m).wait_recv()
                add = macc[...]
                for i in range(PER):
                    h = (FORWARD + m) * PER + i
                    grad = mrecv[m * PER + i].astype(F32)
                    dn[h] = grad
                    add += grad * x_of(h)
                macc[...] = add
                return 0

            lax.fori_loop(0, moved, theirs, 0)
            finish()
            total_copy.wait_recv()
            write_gains()

            def sent(c, _):
                ret_copy(c).wait_send()
                return 0

            lax.fori_loop(0, FORWARD, sent, 0)

            def given(m, _):
                nq_copy(m).wait_send()
                gq_copy(m).wait_send()
                return 0

            lax.fori_loop(0, moved, given, 0)
            flag_copy.wait_send()
            for k in HIGH_GROUPS:
                sums_sent(k)

        def last(c, _):
            g_copy(c).wait_send()
            out_copy(c).wait()
            return 0

        lax.fori_loop(0, chunks, last, 0)

    dma = pltpu.SemaphoreType.DMA
    whole = pltpu.VMEM((heads, block, HEAD), BF16)
    some = pltpu.VMEM((moved * PER, block, HEAD), BF16)
    tiles = (chunks, 8, HEAD)
    scratch = [
        pltpu.SMEM((1, 1), jnp.int32),
        pltpu.VMEM((block, channels), BF16),
        pltpu.VMEM((block, channels), BF16),
        pltpu.VMEM((3, 1, channels), F32),
        whole, whole, whole, whole,
        some,
        pltpu.VMEM((block, moved * width), BF16),
        some, some,
        pltpu.VMEM((2, 8, HEAD), F32),
        pltpu.VMEM((heads, block, HEAD), F32),
        pltpu.VMEM((block, HEAD), F32),
        pltpu.VMEM((block, HEAD), F32),
        pltpu.VMEM((block, channels), BF16),
        pltpu.VMEM(tiles, F32),
        pltpu.VMEM((n_seq, *tiles), F32),
        pltpu.VMEM(tiles, F32),
        pltpu.VMEM((chips, *tiles), F32),
        pltpu.VMEM(tiles, F32),
        dma((3,)), dma((chunks,)),
        dma((chunks,)), dma((chunks,)), dma((chunks,)), dma((chunks,)),
        dma((chunks,)), dma((chunks,)),
        dma((moved,)), dma((moved,)), dma((moved,)), dma((moved,)), dma((moved,)), dma((moved,)),
        dma((2,)), dma((2,)),
        dma((groups, half)), dma((groups, n_seq)), dma((groups,)), dma((groups,)),
        dma((groups, chips)), dma((groups, chips)),
    ]
    return pl.pallas_call(
        kernel,
        out_shape=(
            jax.ShapeDtypeStruct((1, 1, block, channels), BF16),
            jax.ShapeDtypeStruct((3, 1, channels), F32),
        ),
        in_specs=[pl.BlockSpec(memory_space=pltpu.HBM)] * 4,
        out_specs=(
            pl.BlockSpec(memory_space=pl.ANY),
            pl.BlockSpec(memory_space=pltpu.VMEM),
        ),
        scratch_shapes=scratch,
        compiler_params=pltpu.CompilerParams(
            collective_id=0, has_side_effects=True, vmem_limit_bytes=32 << 20
        ),
    )


def solution(mesh):
    def local(section_inputs, grad_send, gains, layout):
        call = make_kernel(
            mesh.shape["seq"], mesh.shape["dp"], mesh.shape["section"],
            section_inputs.shape[-1], section_inputs.shape[-2],
        )
        operands = [section_inputs, grad_send, jnp.swapaxes(gains, 0, 1)]
        operands = [pltpu.with_memory_space_constraint(v, pltpu.HBM) for v in operands]
        input_grad, gain_rows = call(layout, *operands)
        return input_grad, jnp.swapaxes(gain_rows, 0, 1)

    in_specs = (
        P("section", "dp", "seq", None),
        P("section", "dp", "seq", None),
        P("section", None, None),
        P("section", "seq"),
    )
    out_specs = (P("section", "dp", "seq", None), P("section", None, None))
    return jax.shard_map(local, mesh=mesh, in_specs=in_specs, out_specs=out_specs, check_vma=False)
```

```python
import math

import jax
import jax.numpy as jnp
from jax import lax
from jax.experimental import pallas as pl
from jax.experimental.pallas import tpu as pltpu
from jax.sharding import PartitionSpec as P

MESH = pl.DeviceIdType.MESH
HEAD = 128
EPS = 1e-06
NEG = -1e30
PER = 2
FORWARD = 8
GROUPS = ((0, 5), (5, 7), (7, 8), (0, 8), (8, 10))
HIGH_GROUPS, LOW_GROUPS = (0, 1, 2), (3, 4)
F32 = jnp.float32
BF16 = jnp.bfloat16


def dot(left, right, dims):
    return lax.dot_general(left, right, (dims, ((), ())), preferred_element_type=F32)


def make_kernel(n_seq, n_dp, n_section, channels, block):
    heads = channels // HEAD
    chunks = heads // PER
    moved = chunks - FORWARD
    width = PER * HEAD
    half = n_seq // 2
    chips = n_dp // 2
    groups = len(GROUPS)
    tokens_all = n_dp * n_seq * block
    factor = 1.0 / math.sqrt(HEAD)

    def kernel(
        layout_hbm, x_hbm, g_hbm, gains_hbm, out_hbm, gain_out,
        layout, xv, gv, gains, nrm, far, rsend, rrecv, nq, gq, msend, mrecv, flag,
        dn, scale, macc, ov, gg, zbuf, pair, xbuf, fin,
        load_sem, out_sem, g_s, g_r, f_s, f_r, r_s, r_r,
        nq_s, nq_r, gq_s, gq_r, m_s, m_r, one_s, one_r, z_s, z_r, sib_s, sib_r, x_s, x_r, up, go,
    ):
        z = lax.axis_index("seq")
        d = lax.axis_index("dp")
        s = lax.axis_index("section")
        high = z >= half
        low = z < half
        partner = lax.rem(z + half, n_seq)
        chip = d // 2
        core = lax.rem(d, 2)
        sibling = 2 * chip + 1 - core
        below = lax.rem(s + n_section - 1, n_section)
        above = lax.rem(s + 1, n_section)

        def remote(src, dst, send, recv, where):
            return pltpu.make_async_remote_copy(
                src_ref=src, dst_ref=dst, send_sem=send, recv_sem=recv,
                device_id=where, device_id_type=MESH,
            )

        bar = pltpu.get_barrier_semaphore()

        def greet(where):
            pl.semaphore_signal(bar, inc=1, device_id=where, device_id_type=MESH)

        greet({"seq": partner})
        load_x = pltpu.make_async_copy(x_hbm.at[0, 0], xv, load_sem.at[0])
        load_x.start()
        load_gains = pltpu.make_async_copy(gains_hbm, gains, load_sem.at[1])
        load_gains.start()
        load_layout = pltpu.make_async_copy(layout_hbm, layout, load_sem.at[2])
        load_layout.start()
        greet({"section": above})

        @pl.when(low & (z != 0))
        def _():
            greet({"dp": sibling})
            for p in range(chips):
                @pl.when(chip != p)
                def _():
                    greet({"dp": 2 * p + core})

        @pl.when(low)
        def _():
            greet({"section": above, "seq": partner})
            for j in range(half):
                @pl.when(z != j)
                def _():
                    greet({"seq": j})
                    greet({"seq": half + j})

        def lanes(h):
            return pl.ds(pl.multiple_of(h * HEAD, HEAD), HEAD)

        def wide(c):
            return pl.ds(pl.multiple_of(c * width, width), width)

        load_x.wait()

        def square(h, acc):
            v = xv[:, lanes(h)].astype(F32)
            return acc + v * v

        squares = lax.fori_loop(0, heads, square, jnp.zeros((block, HEAD), F32))
        mean = jnp.sum(squares, axis=1, keepdims=True) / channels
        scale[...] = jnp.broadcast_to(lax.rsqrt(mean + EPS), (block, HEAD))

        def norm(h, _):
            nrm[h] = (xv[:, lanes(h)].astype(F32) * scale[...]).astype(BF16)
            return 0

        lax.fori_loop(0, heads, norm, 0)
        load_gains.wait()
        load_layout.wait()
        flag[0] = jnp.full((8, HEAD), layout[0, 0], jnp.int32).astype(F32)
        macc[...] = jnp.zeros_like(macc)
        gg[...] = jnp.zeros_like(gg)

        pl.semaphore_wait(bar, jnp.where(high, half + 2, jnp.where(z == 0, half + 1, half + 1 + chips)))

        def far_copy(c):
            part = pl.ds(c * PER, PER)
            return remote(nrm.at[part], far.at[part], f_s.at[c], f_r.at[c], {"seq": partner})

        def ret_copy(c):
            part = pl.ds(c * PER, PER)
            return remote(rsend.at[part], rrecv.at[part], r_s.at[c], r_r.at[c], {"seq": partner})

        def nq_copy(m):
            return remote(
                nrm.at[pl.ds((FORWARD + m) * PER, PER)], nq.at[pl.ds(m * PER, PER)],
                nq_s.at[m], nq_r.at[m], {"seq": partner},
            )

        def gq_copy(m):
            return remote(
                g_hbm.at[0, 0, :, wide(FORWARD + m)], gq.at[:, wide(m)],
                gq_s.at[m], gq_r.at[m], {"section": below, "seq": partner},
            )

        def back_copy(m):
            part = pl.ds(m * PER, PER)
            return remote(msend.at[part], mrecv.at[part], m_s.at[m], m_r.at[m], {"seq": partner})

        def g_copy(c):
            part = wide(c)
            return remote(
                g_hbm.at[0, 0, :, part], gv.at[:, part], g_s.at[c], g_r.at[c], {"section": below}
            )

        flag_copy = remote(flag.at[0], flag.at[1], one_s.at[0], one_r.at[0], {"seq": partner})

        def total_copy(i, part):
            return remote(
                fin.at[part], fin.at[part], one_s.at[1 + i], one_r.at[1 + i], {"seq": partner}
            )

        def tell_peers():
            pl.semaphore_signal(up, inc=1, device_id={"dp": sibling}, device_id_type=MESH)
            for p in range(chips):
                @pl.when(chip != p)
                def _():
                    pl.semaphore_signal(
                        up, inc=1, device_id={"dp": 2 * p + core}, device_id_type=MESH
                    )

        def tell(where):
            pl.semaphore_signal(go, inc=1, device_id={"seq": where}, device_id_type=MESH)

        @pl.when(low)
        def _():
            def send(c, _):
                far_copy(c).start()
                return 0

            lax.fori_loop(0, FORWARD, send, 0)

        @pl.when(low & (z != 0))
        def _():
            tell_peers()

        @pl.when(high)
        def _():
            flag_copy.start()

            def send(m, _):
                nq_copy(m).start()
                gq_copy(m).start()
                return 0

            lax.fori_loop(0, moved, send, 0)

        def send_g(c, _):
            g_copy(c).start()
            return 0

        lax.fori_loop(0, chunks, send_g, 0)

        def head(h, own, cot, other=None, flags=None):
            part = lanes(h)
            g0 = gains[0, :, part]
            g1 = gains[1, :, part]
            g2 = gains[2, :, part]
            n = own.astype(F32)
            q = (n * g0).astype(BF16)
            k = (n * g1).astype(BF16)
            v = (n * g2).astype(BF16)
            key = lax.broadcasted_iota(jnp.int32, (block, block), 0)
            query = lax.broadcasted_iota(jnp.int32, (block, block), 1)
            if other is not None:
                nf = other.astype(F32)
                k = jnp.concatenate([k, (nf * g1).astype(BF16)], axis=0)
                v = jnp.concatenate([v, (nf * g2).astype(BF16)], axis=0)
            scores = dot(k, q, ((1,), (1,))) * factor
            dprobs = dot(v, cot, ((1,), (1,)))
            near = jnp.where(key <= query, scores[:block], NEG)
            if other is not None:
                scores = jnp.concatenate([near, jnp.where(flags > 0.5, scores[block:], NEG)], axis=0)
            else:
                scores = near
            top = jnp.max(scores, axis=0, keepdims=True)
            weights = jnp.exp(scores - top)
            probs = weights * (1.0 / jnp.sum(weights, axis=0, keepdims=True))
            delta = jnp.sum(probs * dprobs, axis=0, keepdims=True)
            dscores = (probs * (dprobs - delta) * factor).astype(BF16)
            d_query = dot(dscores, k, ((0,), (0,)))
            d_key = dot(dscores, q, ((1,), (0,)))
            d_value = dot(probs.astype(BF16), cot, ((1,), (0,)))
            own_key, own_value = d_key[:block], d_value[:block]
            key_terms = own_key * n
            value_terms = own_value * n
            d_far = None
            if other is not None:
                far_key, far_value = d_key[block:], d_value[block:]
                key_terms += far_key * nf
                value_terms += far_value * nf
                d_far = far_key * g1 + far_value * g2
            sums = [
                jnp.sum(term, axis=0, keepdims=True) for term in (d_query * n, key_terms, value_terms)
            ]
            return d_query * g0 + own_key * g1 + own_value * g2, d_far, sums

        def put_sums(c, i, sums):
            for r in range(3):
                gg[c, pl.ds(3 * i + r, 1), :] = sums[r]

        def x_of(h):
            return xv[:, lanes(h)].astype(F32)

        def tiles_of(k):
            return pl.ds(GROUPS[k][0], GROUPS[k][1] - GROUPS[k][0])

        def sib_copy(k):
            part = tiles_of(k)
            return remote(gg.at[part], pair.at[part], sib_s.at[k], sib_r.at[k], {"dp": sibling})

        def x_copy(k, p, source):
            part = tiles_of(k)
            return remote(
                xbuf.at[source, part], xbuf.at[source, part],
                x_s.at[k, p], x_r.at[k, source], {"dp": 2 * p + core},
            )

        def z_copy(k, j, source):
            part = tiles_of(k)
            return remote(
                zbuf.at[source, part], zbuf.at[source, part],
                z_s.at[k, j], z_r.at[k, source], {"seq": j},
            )

        def over_cores(k):
            part = tiles_of(k)
            sib_copy(k).wait_recv()
            xbuf[chip, part] = gg[part] + pair[part]
            for p in range(chips):
                @pl.when(chip != p)
                def _():
                    x_copy(k, p, chip).start()

        def over_x(k):
            part = tiles_of(k)
            for p in range(chips):
                @pl.when(chip != p)
                def _():
                    x_copy(k, 0, p).wait_recv()
            zbuf[z, part] = jnp.sum(xbuf[:, part], axis=0)
            for j in range(half):
                @pl.when(z != j)
                def _():
                    z_copy(k, j, z).start()

        late = tiles_of(HIGH_GROUPS[-1])

        def add_up(part, sources):
            ratio = 1.0 / math.sqrt(tokens_all)
            fin[part] = jnp.sum(zbuf[pl.ds(0, sources), part], axis=0) * ratio

        def over_z():
            for k in HIGH_GROUPS[:-1]:
                for j in range(half, n_seq):
                    z_copy(k, 0, j).wait_recv()
            for k in LOW_GROUPS:
                for j in range(half):
                    @pl.when(z != j)
                    def _():
                        z_copy(k, 0, j).wait_recv()
            add_up(pl.ds(0, GROUPS[HIGH_GROUPS[-1]][0]), n_seq)
            add_up(pl.ds(FORWARD, moved), half)
            total_copy(0, pl.ds(0, GROUPS[HIGH_GROUPS[-1]][0])).start()
            total_copy(1, pl.ds(FORWARD, moved)).start()
            for j in range(half, n_seq):
                z_copy(HIGH_GROUPS[-1], 0, j).wait_recv()
            add_up(late, n_seq)
            total_copy(2, late).start()

        def totals(act):
            act(total_copy(0, pl.ds(0, GROUPS[HIGH_GROUPS[-1]][0])))
            act(total_copy(1, pl.ds(FORWARD, moved)))
            act(total_copy(2, late))

        def sums_sent(k):
            sib_copy(k).wait_send()
            for p in range(chips):
                @pl.when(chip != p)
                def _():
                    x_copy(k, p, chip).wait_send()
            for j in range(half):
                @pl.when(z != j)
                def _():
                    z_copy(k, j, z).wait_send()

        def write_gains():
            for c in range(chunks):
                for i in range(PER):
                    for r in range(3):
                        part = pl.ds((c * PER + i) * HEAD, HEAD)
                        gain_out[r, :, part] = fin[c, pl.ds(3 * i + r, 1), :]

        def out_copy(c):
            part = wide(c)
            return pltpu.make_async_copy(
                ov.at[:, part], out_hbm.at[0, 0, :, part], out_sem.at[c]
            )

        def finish():
            inv = scale[...]
            total = jnp.sum(macc[...], axis=1, keepdims=True) / channels
            pull = inv * inv * inv * total

            def body(c, _):
                for i in range(PER):
                    h = c * PER + i
                    part = lanes(h)
                    ov[:, part] = (
                        gv[:, part].astype(F32) + inv * dn[h] - x_of(h) * pull
                    ).astype(BF16)
                out_copy(c).start()
                return 0

            lax.fori_loop(0, chunks, body, 0)

        @pl.when(low)
        def _():
            def near(c, _):
                g_copy(c).wait_recv()

                @pl.when((z != 0) & (c == 2))
                def _():
                    pl.semaphore_wait(up, chips)
                    tell(partner)

                @pl.when((z == 1) & (c == 2))
                def _():
                    tell(0)

                @pl.when((z == 0) & (c == 4))
                def _():
                    pl.semaphore_wait(go, 1)
                    tell_peers()

                @pl.when((z == 0) & (c == 7))
                def _():
                    pl.semaphore_wait(up, chips)
                    tell(partner)

                add = macc[...]
                for i in range(PER):
                    h = c * PER + i
                    grad, _far, sums = head(h, nrm[h], gv[:, lanes(h)])
                    dn[h] = grad
                    put_sums(c, i, sums)
                    add += grad * x_of(h)
                macc[...] = add
                return 0

            lax.fori_loop(0, chunks, near, 0)
            sib_copy(LOW_GROUPS[0]).start()
            flag_copy.wait_recv()

            def mine(m, _):
                nq_copy(m).wait_recv()
                gq_copy(m).wait_recv()
                add = macc[...]
                c = FORWARD + m
                for i in range(PER):
                    h = c * PER + i
                    grad, d_far, sums = head(
                        h, nq[m * PER + i], gq[:, lanes(m * PER + i)], nrm[h], flag[1, pl.ds(0, 1), :]
                    )
                    msend[m * PER + i] = grad.astype(BF16)
                    dn[h] += d_far
                    put_sums(c, i, [gg[c, pl.ds(3 * i + r, 1), :] + sums[r] for r in range(3)])
                    add += d_far * x_of(h)
                back_copy(m).start()
                macc[...] = add

                @pl.when(m == 0)
                def _():
                    over_cores(LOW_GROUPS[0])

                return 0

            lax.fori_loop(0, moved, mine, 0)
            sib_copy(LOW_GROUPS[1]).start()
            over_cores(LOW_GROUPS[1])
            for k in LOW_GROUPS:
                over_x(k)

            def back(c, _):
                ret_copy(c).wait_recv()
                add = macc[...]
                for i in range(PER):
                    h = c * PER + i
                    more = rrecv[h].astype(F32)
                    dn[h] += more
                    add += more * x_of(h)
                macc[...] = add
                return 0

            lax.fori_loop(0, FORWARD, back, 0)
            finish()
            over_z()
            write_gains()

            def sent(c, _):
                far_copy(c).wait_send()
                return 0

            lax.fori_loop(0, FORWARD, sent, 0)

            def given(m, _):
                back_copy(m).wait_send()
                return 0

            lax.fori_loop(0, moved, given, 0)
            for k in LOW_GROUPS:
                sums_sent(k)
            totals(lambda copy: copy.wait_send())

        @pl.when(high)
        def _():
            first = z == half

            def both(c, _):
                for k in HIGH_GROUPS[:-1]:
                    @pl.when(~first & (c == GROUPS[k][1]))
                    def _():
                        over_cores(k)

                g_copy(c).wait_recv()
                far_copy(c).wait_recv()
                add = macc[...]
                for i in range(PER):
                    h = c * PER + i
                    grad, d_far, sums = head(
                        h, nrm[h], gv[:, lanes(h)], far[h], flag[0, pl.ds(0, 1), :]
                    )
                    dn[h] = grad
                    rsend[h] = d_far.astype(BF16)
                    put_sums(c, i, sums)
                    add += grad * x_of(h)
                ret_copy(c).start()
                macc[...] = add

                @pl.when(~first & (c == GROUPS[0][1] - 1))
                def _():
                    pl.semaphore_wait(go, 1)
                    sib_copy(0).start()

                @pl.when(~first & (c == GROUPS[1][1] - 1))
                def _():
                    sib_copy(1).start()

                return 0

            lax.fori_loop(0, FORWARD, both, 0)

            @pl.when(first)
            def _():
                pl.semaphore_wait(go, 1)
                for k in HIGH_GROUPS[:-1]:
                    sib_copy(k).start()

            sib_copy(2).start()
            over_cores(2)

            @pl.when(first)
            def _():
                for k in HIGH_GROUPS[:-1]:
                    over_cores(k)

            for k in HIGH_GROUPS:
                over_x(k)

            def theirs(m, _):
                back_copy(m).wait_recv()
                g_copy(FORWARD + m).wait_recv()
                add = macc[...]
                for i in range(PER):
                    h = (FORWARD + m) * PER + i
                    grad = mrecv[m * PER + i].astype(F32)
                    dn[h] = grad
                    add += grad * x_of(h)
                macc[...] = add
                return 0

            lax.fori_loop(0, moved, theirs, 0)
            finish()
            totals(lambda copy: copy.wait_recv())
            write_gains()

            def sent(c, _):
                ret_copy(c).wait_send()
                return 0

            lax.fori_loop(0, FORWARD, sent, 0)

            def given(m, _):
                nq_copy(m).wait_send()
                gq_copy(m).wait_send()
                return 0

            lax.fori_loop(0, moved, given, 0)
            flag_copy.wait_send()
            for k in HIGH_GROUPS:
                sums_sent(k)

        def last(c, _):
            g_copy(c).wait_send()
            out_copy(c).wait()
            return 0

        lax.fori_loop(0, chunks, last, 0)

    dma = pltpu.SemaphoreType.DMA
    whole = pltpu.VMEM((heads, block, HEAD), BF16)
    some = pltpu.VMEM((moved * PER, block, HEAD), BF16)
    tiles = (chunks, 8, HEAD)
    scratch = [
        pltpu.SMEM((1, 1), jnp.int32),
        pltpu.VMEM((block, channels), BF16),
        pltpu.VMEM((block, channels), BF16),
        pltpu.VMEM((3, 1, channels), F32),
        whole, whole, whole, whole,
        some,
        pltpu.VMEM((block, moved * width), BF16),
        some, some,
        pltpu.VMEM((2, 8, HEAD), F32),
        pltpu.VMEM((heads, block, HEAD), F32),
        pltpu.VMEM((block, HEAD), F32),
        pltpu.VMEM((block, HEAD), F32),
        pltpu.VMEM((block, channels), BF16),
        pltpu.VMEM(tiles, F32),
        pltpu.VMEM((n_seq, *tiles), F32),
        pltpu.VMEM(tiles, F32),
        pltpu.VMEM((chips, *tiles), F32),
        pltpu.VMEM(tiles, F32),
        dma((3,)), dma((chunks,)),
        dma((chunks,)), dma((chunks,)), dma((chunks,)), dma((chunks,)),
        dma((chunks,)), dma((chunks,)),
        dma((moved,)), dma((moved,)), dma((moved,)), dma((moved,)), dma((moved,)), dma((moved,)),
        dma((4,)), dma((4,)),
        dma((groups, half)), dma((groups, n_seq)), dma((groups,)), dma((groups,)),
        dma((groups, chips)), dma((groups, chips)),
        pltpu.SemaphoreType.REGULAR, pltpu.SemaphoreType.REGULAR,
    ]
    return pl.pallas_call(
        kernel,
        out_shape=(
            jax.ShapeDtypeStruct((1, 1, block, channels), BF16),
            jax.ShapeDtypeStruct((3, 1, channels), F32),
        ),
        in_specs=[pl.BlockSpec(memory_space=pltpu.HBM)] * 4,
        out_specs=(
            pl.BlockSpec(memory_space=pl.ANY),
            pl.BlockSpec(memory_space=pltpu.VMEM),
        ),
        scratch_shapes=scratch,
        compiler_params=pltpu.CompilerParams(
            collective_id=0, has_side_effects=True, vmem_limit_bytes=32 << 20
        ),
    )


def solution(mesh):
    def local(section_inputs, grad_send, gains, layout):
        call = make_kernel(
            mesh.shape["seq"], mesh.shape["dp"], mesh.shape["section"],
            section_inputs.shape[-1], section_inputs.shape[-2],
        )
        operands = [section_inputs, grad_send, jnp.swapaxes(gains, 0, 1)]
        operands = [pltpu.with_memory_space_constraint(v, pltpu.HBM) for v in operands]
        input_grad, gain_rows = call(layout, *operands)
        return input_grad, jnp.swapaxes(gain_rows, 0, 1)

    in_specs = (
        P("section", "dp", "seq", None),
        P("section", "dp", "seq", None),
        P("section", None, None),
        P("section", "seq"),
    )
    out_specs = (P("section", "dp", "seq", None), P("section", None, None))
    return jax.shard_map(local, mesh=mesh, in_specs=in_specs, out_specs=out_specs, check_vma=False)
```
